32 devices in a mesh: groups: 2 (over y), loop: 8 (over z, core), rep: 2 (over x).
Axes of the slice: x: 2, y: 2, z: 4, core: 2. Of those that a mesh axis runs over, the one named last changes fastest.
Arguments:
- documents: bfloat16 [16384, 1024], P(('groups', 'loop')), parts along dimension 0, may hold values from -6 to 6
- block_ids: int32 [16384, 3], P(('groups', 'loop')), parts along dimension 0, may hold values from 0 to 7, all different within a row; in each aligned block of 1024 rows (0 to 1023, 1024 to 2047, ...) at most 768 rows name the same one
- label_weight: bfloat16 [8192, 1024], P(('loop', 'rep')), may hold values from -0.1875 to 0.1875
- label_bias: bfloat16 [8192], P(('loop', 'rep')), may hold values from -2 to 1
- label_embed: bfloat16 [8192, 768], P(('loop', 'rep')), may hold values from -6 to 6
Outputs:
- pooled: bfloat16 [16384, 768], P(('groups', 'loop', 'rep')), parts along dimension 0
The draws below stay inside these ranges and needn't reach their ends.
There are 2 independent parts, one for each index of `groups`. The reference program is written for one: setup_inputs(seed, part) draws one part's arguments, and reference() takes and returns one part's arrays. A program takes and returns all parts, laid end to end along the dimension named above; an argument that names none is the same for every part. Nothing has to cross between parts.
Inputs may be any that keep to these rules, and one draw needn't show every extreme that they name: `block_ids`: each row names 3 different label blocks; every block is named by some row; among the 1024 rows of one index of loop no block is named by more than 768 rows.
All inputs are finite; a program needn't handle non-finite values.
Results may differ from the reference program's by a relative error of at most 0.0048.
Values may be sent and summed in bfloat16 or wider, within the bound.
No kernel may reach another device: no remote copies, remote signals or barrier semaphores. Data moves between devices by JAX's collectives and lax.ppermute only.
A program may use at most 192 MiB of HBM per device.

```python
import math
import jax
import jax.numpy as jnp
import numpy as np
from jax import lax

D = 1024
DE = 768
DOC_DEV = 1024
K = 3
NBLK = 8
BLK = 1024
LABELS = 8192
CAP = 768
DOCS = 8192
N_LOOP = 8


def steps_of(key, shape, cuts, smallest, top_value):
    def one(axis_at, parts):
        draws = jax.random.uniform(jax.random.fold_in(jax.random.fold_in(key, 6), axis_at), (parts,), jnp.float32, smallest / len(cuts), top_value / len(cuts))
        return jnp.repeat(jnp.exp(draws), shape[axis_at] // parts).reshape((-1,) + (1,) * (len(shape) - axis_at - 1))

    factor_of = one(*cuts[0])
    for cut in cuts[1:]:
        factor_of = factor_of * one(*cut)
    return factor_of


def assign_block(rng, own, number, rows, count, top, bound, slope):
    ranking = jax.random.permutation(rng, count)
    crowded, common = shares(count, rows * top, bound, slope, True), shares(count, rows * top, bound, slope, False)
    places = jnp.arange(count)

    def named(lengths, offset_by):
        used = int((lengths > 0).sum())
        fixed = max(1, used // 4)
        shifted = fixed + (places - fixed + offset_by * (used - fixed)) % max(1, count - fixed)
        return jnp.zeros((count,), jnp.int32).at[ranking[jnp.where(places < fixed, places, shifted)]].set(jnp.asarray(lengths, jnp.int32))

    lengths = jnp.where(number % 4 == 0, named(crowded, number // 4), named(common, number - number // 4 - 1))
    mixed = jax.random.permutation(jax.random.fold_in(own, 3), count)
    donor, taker = mixed[0:count // 2 * 2:2], mixed[1:count // 2 * 2:2]
    room = jnp.minimum(lengths[donor] - 1, bound - lengths[taker]) // 2
    room = jnp.where((donor == ranking[0]) | (taker == ranking[0]) | (lengths[taker] == 0), 0, jnp.maximum(room, 0))
    shifted = jax.random.randint(jax.random.fold_in(own, 4), (count // 2,), 0, 1 << 20) % (room + 1)
    lengths = lengths.at[donor].add(-shifted).at[taker].add(shifted)
    labels = jnp.searchsorted(jnp.cumsum(lengths), jnp.arange(rows * top), side="right").astype(jnp.int32)
    grid = labels.reshape(top, rows).T
    grid = grid[jax.random.permutation(jax.random.fold_in(own, 1), rows)]
    offset_by = jax.random.randint(jax.random.fold_in(own, 2), (rows, 1), 0, top)
    return jnp.take_along_axis(grid, (jnp.arange(top)[None, :] + offset_by) % top, axis=1)


def shares(amount, total, limit, lean, full):
    portions = [(1 << 20) // math.isqrt(rank ** lean) + 1 for rank in range(1, amount + 1)]
    largest = limit if full else min(limit, max(-(-total // amount), total * portions[0] // sum(portions)))
    least = 1 if total - largest >= amount - 1 else 0
    holding, rest = [largest] + [least] * (amount - 1), total - largest - least * (amount - 1)
    while rest > 0:
        free = [i for i in range(1, amount) if holding[i] < largest] or [i for i in range(1, amount) if holding[i] < limit]
        whole, left = sum([portions[i] for i in free]), rest
        for i in free:
            extra = min(limit - holding[i], max(1, left * portions[i] // whole), rest)
            holding[i] = holding[i] + extra
            rest = rest - extra
    return np.array(holding)


def centred(stream_key, extent, scale, limit, pieces=(), kind=jnp.bfloat16):
    result = scale * jax.random.normal(stream_key, extent, jnp.float32)
    if pieces:
        result = result * steps_of(stream_key, extent, pieces, -0.22, 0.18)
    return jnp.clip(result, -limit, limit).astype(kind)


def setup_inputs(seed: int = 0, part: int = 0) -> dict:
    streams_of = jax.random.split(jax.random.key(seed), 6)
    own_keys = jax.random.split(jax.random.fold_in(streams_of[5], part), 6)
    documents = centred(own_keys[0], (DOCS, D), 1.0, 6.0, ((0, 8),))
    block_ids_keys = jax.random.split(jax.random.fold_in(own_keys[1], 1), DOCS // DOC_DEV)
    block_ids_turns = jax.random.permutation(jax.random.fold_in(own_keys[1], 3), DOCS // DOC_DEV)
    block_ids = jax.vmap(lambda own, number: assign_block(jax.random.fold_in(own_keys[1], 2), own, number, DOC_DEV, NBLK, K, CAP, 1))(block_ids_keys, block_ids_turns).reshape((DOCS, K))
    label_weight = centred(streams_of[2], (LABELS, D), D ** -0.5, 0.1875, ((0, 16),))
    label_bias = jnp.clip(-2.0 + 3.0 * jax.random.uniform(streams_of[3], (LABELS,), jnp.float32) ** steps_of(streams_of[3], (LABELS,), ((0, 16),), -0.2, 0.2), -2.0, 1.0).astype(jnp.bfloat16)
    label_embed = centred(streams_of[4], (LABELS, DE), 1.0, 6.0, ((0, 16),))
    return dict(documents=documents, block_ids=block_ids, label_weight=label_weight, label_bias=label_bias, label_embed=label_embed)


def slot_table(ids, block_count, slot_count):
    doc_count = ids.shape[0]
    blocks = jnp.arange(block_count, dtype=jnp.int32)
    member = jnp.any(ids[:, :, None] == blocks[None, None, :], axis=1).astype(jnp.int32)
    rank = (jnp.cumsum(member, axis=0) - 1).astype(jnp.int32)
    rows = jnp.where(member > 0, rank, slot_count).astype(jnp.int32)
    cols = jnp.broadcast_to(blocks[None, :], rows.shape)
    owners = jnp.broadcast_to(jnp.arange(doc_count, dtype=jnp.int32)[:, None], rows.shape)
    table = jnp.full((block_count, slot_count + 1), doc_count, jnp.int32).at[cols, rows].set(owners)
    return table[:, :slot_count]

def reference(documents, block_ids, label_weight, label_bias, label_embed):
    doc_groups = documents.reshape(N_LOOP, DOC_DEV, D)
    id_groups = block_ids.reshape(N_LOOP, DOC_DEV, K)
    weight_blocks = label_weight.reshape(NBLK, BLK, D)
    bias_blocks = label_bias.reshape(NBLK, BLK)
    embed_blocks = label_embed.reshape(NBLK, BLK, DE)

    def one_group(pair):
        docs, ids = pair
        table = slot_table(ids, NBLK, CAP)

        def one_block(carry, index):
            slots = table[index]
            rows = docs[jnp.minimum(slots, DOC_DEV - 1)]
            logits = jnp.dot(rows, weight_blocks[index].T, preferred_element_type=jnp.float32)
            logits = logits + bias_blocks[index].astype(jnp.float32)[None, :]
            weights = jax.nn.sigmoid(logits).astype(jnp.bfloat16)
            mix = jnp.dot(weights, embed_blocks[index], preferred_element_type=jnp.float32)
            sums = lax.optimization_barrier(jnp.sum(weights.astype(jnp.float32), axis=1))
            mixture = carry[0].at[slots].add(mix, mode='drop')
            weight_sum = carry[1].at[slots].add(sums, mode='drop')
            return ((mixture, weight_sum), None)
        start = (jnp.zeros((DOC_DEV, DE), jnp.float32), jnp.zeros((DOC_DEV,), jnp.float32))
        totals, unused = lax.scan(one_block, start, jnp.arange(NBLK, dtype=jnp.int32))
        mixture, weight_sum = totals
        return (mixture / jnp.sqrt(1.0 + weight_sum)[:, None]).astype(jnp.bfloat16)
    pooled = lax.map(one_group, (doc_groups, id_groups))
    return pooled.reshape(DOCS, DE)
```

```python
import functools

import jax
import jax.numpy as jnp
from jax import lax
from jax.experimental import pallas as pl
from jax.experimental.pallas import tpu as pltpu
from jax.sharding import PartitionSpec as P

AXES = ("groups", "loop", "rep")
DOC_TILE = 256


def accumulate(spec, table, *refs):
    step, packed, pieces, parts, part_rows, offset, first, final, groups = spec
    docs_ref, ids_ref, bias_ref = refs[:3]
    at = 3
    weight_rows, embed_rows = [], []
    for _ in range(pieces):
        if packed:
            width = docs_ref.shape[1]
            weight_rows.append(refs[at][:, :width])
            embed_rows.append(refs[at][:, width:])
            at += 1
        else:
            weight_rows.append(refs[at][...])
            embed_rows.append(refs[at + 1][...])
            at += 2
    if not first:
        mix_in, sum_in = refs[at], refs[at + 1]
        at += 2
    mix_out, sum_out = refs[at], refs[at + 1]
    group = table[0]
    cores = pieces // parts
    biases, masks = [], []
    ids = ids_ref[...]
    for core in range(cores):
        block = table[1 + 2 * step + core]
        chosen = jnp.max((ids == block).astype(jnp.float32), axis=1, keepdims=True)
        for part in range(parts):
            row = bias_ref[core : core + 1, :]
            rows = weight_rows[core * parts + part].shape[0]
            if parts == 1:
                piece = row
            else:
                owner = lax.rem(group + groups - part, groups)
                piece = row[:, offset : offset + rows]
                for other in range(1, groups):
                    start = other * part_rows + offset
                    piece = jnp.where(owner == other, row[:, start : start + rows], piece)
            biases.append(piece)
            masks.append(jnp.broadcast_to(chosen, (chosen.shape[0], rows)))
    joined = lambda xs, axis: xs[0] if len(xs) == 1 else jnp.concatenate(xs, axis=axis)
    logits = lax.dot_general(
        docs_ref[...],
        joined(weight_rows, 0),
        (((1,), (1,)), ((), ())),
        preferred_element_type=jnp.float32,
    )
    logits = logits + joined(biases, 1)
    weights = (joined(masks, 1) * jax.nn.sigmoid(logits)).astype(jnp.bfloat16)
    mix = jnp.dot(weights, joined(embed_rows, 0), preferred_element_type=jnp.float32)
    sums = jnp.sum(weights.astype(jnp.float32), axis=1, keepdims=True)
    if not first:
        mix = mix + mix_in[...]
        sums = sums + sum_in[...]
    mix_out[...] = mix.astype(mix_out.dtype)
    sum_out[...] = sums


def add_labels(table, docs, ids, bias, pieces, totals, *, step, packed, parts, part_rows, offset, groups, rows_of=None, out_dtype=jnp.float32):
    doc_count, width = docs.shape
    embed_width = pieces[0].shape[1] - width if packed else pieces[1].shape[1]
    first = totals is None
    final = rows_of is not None
    if final:
        tile_of, tiles, tile = rows_of
    else:
        tile = min(DOC_TILE, doc_count)
        tiles = doc_count // tile
        tile_of = lambda i, t: i
    moving = lambda i, t: (tile_of(i, t), 0)
    still = lambda i, t: (0, 0)
    count = len(pieces) if packed else len(pieces) // 2
    spec = (step, packed, count, parts, part_rows, offset, first, final, groups)
    labels = sum(p.shape[0] for p in pieces) // (1 if packed else 2)
    in_specs = [
        pl.BlockSpec((tile, width), moving),
        pl.BlockSpec((tile, ids.shape[1]), moving),
        pl.BlockSpec(bias.shape, still),
    ] + [pl.BlockSpec(p.shape, still) for p in pieces]
    operands = [docs, ids, bias, *pieces]
    aliases = {}
    if not first:
        in_specs += [pl.BlockSpec((tile, embed_width), moving), pl.BlockSpec((tile, 1), moving)]
        operands += list(totals)
        if not final:
            aliases = {len(operands) - 1: 0, len(operands): 1}
    out_map = (lambda i, t: (i, 0)) if final else moving
    return pl.pallas_call(
        functools.partial(accumulate, spec),
        grid_spec=pltpu.PrefetchScalarGridSpec(
            num_scalar_prefetch=1,
            grid=(tiles,),
            in_specs=in_specs,
            out_specs=[pl.BlockSpec((tile, embed_width), out_map), pl.BlockSpec((tile, 1), out_map)],
        ),
        out_shape=[
            jax.ShapeDtypeStruct((tiles * tile, embed_width), out_dtype),
            jax.ShapeDtypeStruct((tiles * tile, 1), jnp.float32),
        ],
        input_output_aliases=aliases,
        compiler_params=pltpu.CompilerParams(vmem_limit_bytes=40 * 1024 * 1024),
        cost_estimate=pl.CostEstimate(
            flops=2 * tiles * tile * labels * (width + embed_width),
            bytes_accessed=2 * tiles * tile * (width + 4 * embed_width) + 2 * labels * (width + embed_width),
            transcendentals=tiles * tile * labels,
        ),
    )(table, *operands)


def per_device(sizes, documents, block_ids, label_weight, label_bias, label_embed):
    groups, loop, reps = sizes
    cores = 2 if loop % 2 == 0 else 1
    chips = loop // cores
    doc_count, width = documents.shape
    shard = label_weight.shape[0]
    part_rows = shard // groups

    def moved(x, to):
        pairs = []
        for g in range(groups):
            for l in range(loop):
                for r in range(reps):
                    g2, z2, c2, r2 = to(g, l // cores, l % cores, r)
                    there = (g2 % groups, (z2 % chips) * cores + c2 % cores, r2 % reps)
                    number = lambda a: (a[0] * loop + a[1]) * reps + a[2]
                    pairs.append((number((g, l, r)), number(there)))
        return lax.ppermute(x, AXES, pairs)

    along = lambda x: moved(x, lambda g, z, c, r: (g, z + 1, c, r))
    across = lambda x, k: moved(x, lambda g, z, c, r: (g + k, z, c, r))
    other_core = lambda x: moved(x, lambda g, z, c, r: (g, z, c + 1, r))
    other_rep = lambda x, k: moved(x, lambda g, z, c, r: (g, z, c, r + k))

    group = lax.axis_index("groups")
    place = lax.axis_index("loop")
    rep = lax.axis_index("rep")
    chip, core = place // cores, place % cores
    entries = [group]
    for step in range(chips):
        for k in range(2):
            entries.append(((chip - step) % chips) * cores + (core + k) % cores)
    entries.append(rep)
    table = jnp.stack(entries).astype(jnp.int32)

    small = max(16, part_rows // 4 // 16 * 16)
    chunks = [(0, part_rows - small), (part_rows - small, small)]
    flying = []
    for offset, rows in chunks:
        start = group * part_rows + offset
        flying.append(
            jnp.concatenate(
                [
                    lax.dynamic_slice_in_dim(label_weight, start, rows, 0),
                    lax.dynamic_slice_in_dim(label_embed, start, rows, 0),
                ],
                axis=1,
            )
        )
    bias_row = label_bias.astype(jnp.float32)[None, :]
    bias = jnp.concatenate([bias_row, other_core(bias_row)], axis=0) if cores == 2 else bias_row

    own = [label_weight, label_embed]
    if cores == 2:
        own += [other_core(label_weight), other_core(label_embed)]
    call = functools.partial(add_labels, table, documents, block_ids)
    common = dict(part_rows=part_rows, groups=groups)
    totals = call(bias, own, None, step=0, packed=False, parts=1, offset=0, **common)
    for step in range(1, chips):
        bias = along(bias)
        for index, (offset, rows) in enumerate(chunks):
            flying[index] = along(flying[index])
            pieces = [flying[index]] + [across(flying[index], k) for k in range(1, groups)]
            if cores == 2:
                pieces += [other_core(p) for p in pieces]
            here = dict(step=step, packed=True, parts=groups, offset=offset, **common)
            if step < chips - 1 or index < len(chunks) - 1:
                totals = call(bias, pieces, totals, **here)
    tile_docs = doc_count // reps
    tile = min(DOC_TILE, tile_docs)
    subs = tile_docs // tile
    last = table.shape[0] - 1
    away_of = lambda i, t: lax.rem(t[last] + 1 + i // subs, reps) * subs + i % subs
    home_of = lambda i, t: t[last] * subs + i
    away_mix, away_sum = call(
        bias, pieces, totals, rows_of=(away_of, (reps - 1) * subs, tile), out_dtype=jnp.bfloat16, **here
    )
    home_mix, home_sum = call(bias, pieces, totals, rows_of=(home_of, subs, tile), **here)
    mixture, weight_sum = home_mix, home_sum
    for k in range(1, reps):
        part = slice((k - 1) * tile_docs, k * tile_docs)
        mixture = mixture + other_rep(away_mix[part], k).astype(jnp.float32)
        weight_sum = weight_sum + other_rep(away_sum[part].reshape(-1, 128), k).reshape(-1, 1)
    return (mixture / jnp.sqrt(1.0 + weight_sum)).astype(jnp.bfloat16)


def solution(mesh):
    sizes = tuple(mesh.shape[axis] for axis in AXES)
    return jax.shard_map(
        functools.partial(per_device, sizes),
        mesh=mesh,
        in_specs=(
            P(("groups", "loop"), None),
            P(("groups", "loop"), None),
            P(("loop", "rep"), None),
            P(("loop", "rep")),
            P(("loop", "rep"), None),
        ),
        out_specs=P(("groups", "loop", "rep"), None),
        check_vma=False,
    )
```

```python
import functools

import jax
import jax.numpy as jnp
from jax import lax
from jax.experimental import pallas as pl
from jax.experimental.pallas import tpu as pltpu
from jax.sharding import PartitionSpec as P

AXES = ("groups", "loop", "rep")
DOC_TILE = 256
VMEM_LIMIT = 24 * 1024 * 1024
SHARES = (1, 1)
TIES = {("first", 1): 1, ("mid", 1): 1, ("last", 1): 1}
BIAS_ROWS = 8
COST_NEXT = 4400000000


def joined(xs, axis):
    return xs[0] if len(xs) == 1 else jnp.concatenate(xs, axis=axis)


def column(row):
    return jnp.transpose(jnp.broadcast_to(row[:1], (128, row.shape[1])))[:, :1]


def accumulate(spec, table, bias_ref, *refs):
    step, offsets, parts, part_rows, sets, first, where, reps, received = spec
    count = max(1, len(offsets)) * parts
    labels, refs = refs[: 2 if not offsets else count], refs[2 if not offsets else count :]
    if offsets:
        lead, bias_rows, weight_rows, embed_rows = len(offsets), [], [], []
        for k, ref in enumerate(labels):
            offset = offsets[k % lead]
            rows = ref.shape[0] - (0 if offset else BIAS_ROWS)
            width = sets_width(refs)
            weight_rows.append(ref[:rows, :width])
            embed_rows.append(ref[:rows, width:])
            source = labels[k - k % lead]
            row = source[source.shape[0] - BIAS_ROWS :, :part_rows].astype(jnp.float32)[:1]
            bias_rows.append(row[:, offset : offset + rows])
        bias = joined(bias_rows, 1)
        weight_rows, embed_rows = joined(weight_rows, 0), joined(embed_rows, 0)
    else:
        weight_rows, embed_rows, bias = labels[0][...], labels[1][...], bias_ref[...]
    block, rep = table[1 + step], table[table.shape[0] - 1]
    per_set = 2 + (0 if first else 2) + (2 if received else 0)
    for k in range(sets):
        docs_ref, ids_ref, *rest = refs[k * per_set : (k + 1) * per_set]
        mix_out, sum_out = refs[sets * per_set + 2 * k : sets * per_set + 2 * k + 2]
        held = docs_ref.shape[0] if where == "all" else docs_ref.shape[0] // reps
        tile = min(DOC_TILE, held)
        subs = held // tile

        @pl.loop(0, mix_out.shape[0] // tile)
        def _(i):
            if where == "all":
                source = i
            elif where == "home":
                source = rep * subs + i
            else:
                source = lax.rem(rep + 1 + i // subs, reps) * subs + lax.rem(i, subs)
            from_rows = pl.ds(pl.multiple_of(source * tile, tile), tile)
            to_rows = pl.ds(pl.multiple_of(i * tile, tile), tile)
            chosen = jnp.max((ids_ref[from_rows, :] == block).astype(jnp.float32), axis=1, keepdims=True)
            logits = lax.dot_general(
                docs_ref[from_rows, :], weight_rows, (((1,), (1,)), ((), ())), preferred_element_type=jnp.float32
            )
            weights = (chosen * jax.nn.sigmoid(logits + bias)).astype(jnp.bfloat16)
            mix = jnp.dot(weights, embed_rows, preferred_element_type=jnp.float32)
            sums = jnp.sum(weights.astype(jnp.float32), axis=1, keepdims=True)
            if not first:
                mix = mix + rest[0][from_rows, :]
                sums = sums + rest[1][from_rows, :]
            if received:
                mix = mix + rest[2][to_rows, :].astype(jnp.float32)
                sums = sums + column(rest[3][:, to_rows])
            mix_out[to_rows, :] = mix.astype(mix_out.dtype)
            if sum_out.shape[0] == 8:
                sum_out[:, to_rows] = jnp.transpose(jnp.broadcast_to(sums, (tile, 128)))[:8]
            else:
                sum_out[to_rows, :] = sums


def sets_width(refs):
    return refs[0].shape[1]


def add_labels(table, bias, labels, sets, *, step, offsets, parts, part_rows, reps, where="all", out=jnp.float32):
    embed_width = labels[1].shape[1] if not offsets else labels[0].shape[1] - sets[0][0].shape[1]
    first, received = len(sets[0]) == 2, len(sets[0]) > 4
    spec = (step, offsets, parts, part_rows, len(sets), first, where, reps, received)
    operands = [bias, *labels]
    aliases, out_shape = {}, []
    for k, one in enumerate(sets):
        docs = one[0]
        rows = {"all": docs.shape[0], "home": docs.shape[0] // reps, "away": docs.shape[0] // reps * (reps - 1)}[where]
        if where == "all" and not first:
            aliases[1 + len(operands) + 2] = 2 * k
            aliases[1 + len(operands) + 3] = 2 * k + 1
        operands += one
        out_shape.append(jax.ShapeDtypeStruct((rows, embed_width), out))
        out_shape.append(jax.ShapeDtypeStruct((rows, 1) if out == jnp.float32 else (8, rows), jnp.float32))
    outs = pl.pallas_call(
        functools.partial(accumulate, spec),
        in_specs=[pl.BlockSpec(memory_space=pltpu.SMEM)] + [pl.BlockSpec(memory_space=pltpu.VMEM)] * len(operands),
        out_specs=[pl.BlockSpec(memory_space=pltpu.VMEM)] * len(out_shape),
        out_shape=out_shape,
        input_output_aliases=aliases,
        compiler_params=pltpu.CompilerParams(vmem_limit_bytes=VMEM_LIMIT),
        cost_estimate=pl.CostEstimate(flops=0, bytes_accessed=0, transcendentals=0),
    )(table, *operands)
    return [list(outs[2 * k : 2 * k + 2]) for k in range(len(sets))]


def combine(mix_ref, sum_ref, *refs):
    out_ref, others = refs[-1], list(refs[:-1])
    mix, sums = mix_ref[...], sum_ref[...]
    while others:
        parts, rows = [], 0
        while rows < mix.shape[0]:
            parts.append(others.pop(0)[...].astype(jnp.float32))
            rows += parts[-1].shape[0]
        mix = mix + joined(parts, 0)
        sums = sums + column(others.pop(0)[...])
    out_ref[...] = (mix / jnp.sqrt(1.0 + sums)).astype(out_ref.dtype)


def combined(mix, sums, others):
    return pl.pallas_call(
        combine,
        in_specs=[pl.BlockSpec(memory_space=pltpu.VMEM)] * (2 + len(others)),
        out_specs=pl.BlockSpec(memory_space=pltpu.VMEM),
        out_shape=jax.ShapeDtypeStruct(mix.shape, jnp.bfloat16),
        compiler_params=pltpu.CompilerParams(vmem_limit_bytes=VMEM_LIMIT),
        cost_estimate=pl.CostEstimate(flops=0, bytes_accessed=0, transcendentals=0),
    )(mix, sums, *others)


def pack(spec, table, weight, embed, bias, out, sems):
    offset, rows, part_rows, groups = spec
    width = weight.shape[1]
    group = table[0]
    source = pl.ds(pl.multiple_of(group * part_rows + offset, 16), rows)
    copies = [
        pltpu.make_async_copy(weight.at[source, :], out.at[pl.ds(0, rows), pl.ds(0, width)], sems.at[0]),
        pltpu.make_async_copy(embed.at[source, :], out.at[pl.ds(0, rows), pl.ds(width, embed.shape[1])], sems.at[1]),
    ]
    for copy in copies:
        copy.start()
    if offset == 0:
        row = bias[:, :part_rows]
        for other in range(1, groups):
            row = jnp.where(group == other, bias[:, other * part_rows : (other + 1) * part_rows], row)
        out[rows:, :part_rows] = jnp.broadcast_to(row, (BIAS_ROWS, part_rows)).astype(out.dtype)
        out[rows:, part_rows:] = jnp.zeros((BIAS_ROWS, out.shape[1] - part_rows), out.dtype)
    for copy in copies:
        copy.wait()


def packed_part(table, weight, embed, bias, offset, rows, part_rows, groups, cost):
    width = weight.shape[1] + embed.shape[1]
    return pl.pallas_call(
        functools.partial(pack, (offset, rows, part_rows, groups)),
        in_specs=[pl.BlockSpec(memory_space=pltpu.SMEM)]
        + [pl.BlockSpec(memory_space=pl.ANY)] * 2
        + [pl.BlockSpec(memory_space=pltpu.VMEM)],
        out_specs=pl.BlockSpec(memory_space=pltpu.VMEM),
        out_shape=jax.ShapeDtypeStruct((rows + (0 if offset else BIAS_ROWS), width), weight.dtype),
        scratch_shapes=[pltpu.SemaphoreType.DMA((2,))],
        compiler_params=pltpu.CompilerParams(vmem_limit_bytes=VMEM_LIMIT),
        cost_estimate=pl.CostEstimate(flops=cost, bytes_accessed=0, transcendentals=0),
    )(table, weight, embed, bias)


def per_device(sizes, documents, block_ids, label_weight, label_bias, label_embed):
    groups, loop, reps = sizes
    cores = 2 if loop % 2 == 0 else 1
    chips = loop // cores
    doc_count = documents.shape[0]
    part_rows = label_weight.shape[0] // groups

    def moved(x, to):
        pairs = []
        for g in range(groups):
            for l in range(loop):
                for r in range(reps):
                    g2, z2, c2, r2 = to(g, l // cores, l % cores, r)
                    there = (g2 % groups, (z2 % chips) * cores + c2 % cores, r2 % reps)
                    number = lambda a: (a[0] * loop + a[1]) * reps + a[2]
                    pairs.append((number((g, l, r)), number(there)))
        return lax.ppermute(x, AXES, pairs)

    along = lambda x: moved(x, lambda g, z, c, r: (g, z + 1, c, r))
    across = lambda x, k: moved(x, lambda g, z, c, r: (g + k, z, c, r))
    other_core = lambda x: moved(x, lambda g, z, c, r: (g, z, c + 1, r))
    other_rep = lambda x, k: moved(x, lambda g, z, c, r: (g, z, c, r + k))

    place = lax.axis_index("loop")
    chip, core = place // cores, place % cores
    entries = [lax.axis_index("groups")]
    entries += [((chip - step) % chips) * cores + core for step in range(chips)]
    entries.append(lax.axis_index("rep"))
    table = jnp.stack(entries).astype(jnp.int32)

    total = sum(SHARES)
    cuts = [part_rows * sum(SHARES[:k]) // total // 16 * 16 for k in range(len(SHARES))] + [part_rows]
    chunks = [(a, b - a) for a, b in zip(cuts, cuts[1:])]
    bias = label_bias.astype(jnp.float32)[None, :]
    flying = [
        packed_part(table, label_weight, label_embed, bias, offset, rows, part_rows, groups, COST_NEXT if offset else 0)
        for offset, rows in chunks
    ]
    sets = [[documents, block_ids]]
    if cores == 2:
        sets.append([other_core(documents), other_core(block_ids)])
    call = functools.partial(add_labels, table, bias)
    common = dict(part_rows=part_rows, reps=reps)
    history = [call([label_weight, label_embed], sets, step=0, offsets=(), parts=1, **common)]

    def after(x, step, index):
        back = TIES.get(("last" if step + 1 == chips else "first" if step == 1 else "mid", index))
        if back is None or back > step:
            return x
        x, history[step - back] = lax.optimization_barrier((x, history[step - back]))
        return x

    for step in range(1, chips):
        arrived = []
        for index in range(len(chunks)):
            flying[index] = after(along(flying[index]), step, index)
            arrived.append([flying[index]] + [across(flying[index], k) for k in range(1, groups)])
        labels = [pieces[part] for part in range(groups) for pieces in arrived]
        here = dict(step=step, offsets=tuple(offset for offset, _ in chunks), parts=groups, **common)
        if step + 1 < chips:
            history.append(call(labels, [one + t for one, t in zip(sets, history[-1])], **here))
    held = [one + t for one, t in zip(sets, history[-1])]

    narrow = dict(out=jnp.bfloat16, **here)
    tile_docs = doc_count // reps
    others = []
    away = [held[0]]
    if cores == 2:
        (share,) = call(labels, [held[1]], where="away", **narrow)
        away = [held[0] + [other_core(x) for x in share]]
    (away,) = call(labels, away, where="away", **narrow)
    if cores == 2:
        away, held[1] = lax.optimization_barrier((away, held[1]))
        (share,) = call(labels, [held[1]], where="home", **narrow)
        half = tile_docs // 2
        others += [other_core(share[0][:half]), other_core(share[0][half:]), other_core(share[1])]
    ((home_mix, home_sum),) = call(labels, [held[0]], where="home", **here)
    for k in range(1, reps):
        part = slice((k - 1) * tile_docs, k * tile_docs)
        others += [other_rep(away[0][part], k), other_rep(away[1][:, part], k)]
    return combined(home_mix, home_sum, others)


def solution(mesh):
    sizes = tuple(mesh.shape[axis] for axis in AXES)
    return jax.shard_map(
        functools.partial(per_device, sizes),
        mesh=mesh,
        in_specs=(
            P(("groups", "loop"), None),
            P(("groups", "loop"), None),
            P(("loop", "rep"), None),
            P(("loop", "rep")),
            P(("loop", "rep"), None),
        ),
        out_specs=P(("groups", "loop", "rep"), None),
        check_vma=False,
    )
```

```python
import functools

import jax
import jax.numpy as jnp
from jax import lax
from jax.experimental import pallas as pl
from jax.experimental.pallas import tpu as pltpu
from jax.sharding import PartitionSpec as P

AXES = ("groups", "loop", "rep")
DOC_TILE = 1024
VMEM_LIMIT = 24 * 1024 * 1024
SHARES = (1, 1)
TIES = {("first", 0): 1, ("mid", 1): 1, ("last", 1): 1}
BIAS_ROWS = 8
NEAR = 64
COST_NEXT = 13200000000


def joined(xs, axis):
    return xs[0] if len(xs) == 1 else jnp.concatenate(xs, axis=axis)


def column(row):
    return jnp.transpose(jnp.broadcast_to(row[:1], (128, row.shape[1])))[:, :1]


def accumulate(spec, table, bias_ref, *refs):
    step, pieces, part_rows, sets, first, where, reps, received = spec
    count = max(2, len(pieces))
    labels, refs = refs[:count], refs[count:]
    if pieces:
        width = refs[0].shape[1]
        leads = {part: ref for (part, offset), ref in zip(pieces, labels) if offset == 0}
        bias_rows, weight_rows, embed_rows = [], [], []
        for (part, offset), ref in zip(pieces, labels):
            rows = ref.shape[0] - (0 if offset else BIAS_ROWS)
            weight_rows.append(ref[:rows, :width])
            embed_rows.append(ref[:rows, width:])
            if leads:
                lead = leads[part]
                row = lead[lead.shape[0] - BIAS_ROWS :, :part_rows].astype(jnp.float32)[:1]
            else:
                row = bias_ref[:1, part * part_rows : (part + 1) * part_rows]
            if where == "all" and offset == 0:
                refs[-1][:, part * part_rows : (part + 1) * part_rows] = jnp.broadcast_to(row, (8, part_rows))
            bias_rows.append(row[:, offset : offset + rows])
        bias = joined(bias_rows, 1)
        weight_rows, embed_rows = joined(weight_rows, 0), joined(embed_rows, 0)
    else:
        weight_rows, embed_rows, bias = labels[0][...], labels[1][...], bias_ref[...]
    block, rep = table[1 + step], table[table.shape[0] - 1]
    per_set = 2 + (0 if first else 2) + (2 if received else 0)
    for k in range(sets):
        docs_ref, ids_ref, *rest = refs[k * per_set : (k + 1) * per_set]
        mix_out, sum_out = refs[sets * per_set + 2 * k : sets * per_set + 2 * k + 2]
        held = docs_ref.shape[0] if where == "all" else docs_ref.shape[0] // reps
        tile = min(DOC_TILE, held)
        subs = held // tile

        @pl.loop(0, mix_out.shape[0] // tile)
        def _(i):
            if where == "all":
                source = i
            elif where == "home":
                source = rep * subs + i
            else:
                source = lax.rem(rep + 1 + i // subs, reps) * subs + lax.rem(i, subs)
            from_rows = pl.ds(pl.multiple_of(source * tile, tile), tile)
            to_rows = pl.ds(pl.multiple_of(i * tile, tile), tile)
            chosen = jnp.max((ids_ref[from_rows, :] == block).astype(jnp.float32), axis=1, keepdims=True)
            logits = lax.dot_general(
                docs_ref[from_rows, :], weight_rows, (((1,), (1,)), ((), ())), preferred_element_type=jnp.float32
            )
            weights = (chosen * jax.nn.sigmoid(logits + bias)).astype(jnp.bfloat16)
            mix = jnp.dot(weights, embed_rows, preferred_element_type=jnp.float32)
            sums = jnp.sum(weights.astype(jnp.float32), axis=1, keepdims=True)
            if not first:
                mix = mix + rest[0][from_rows, :]
                sums = sums + rest[1][from_rows, :]
            if received:
                mix = mix + rest[2][to_rows, :].astype(jnp.float32)
                sums = sums + column(rest[3][:, to_rows])
            mix_out[to_rows, :] = mix.astype(mix_out.dtype)
            if sum_out.shape[0] == 8:
                sum_out[:, to_rows] = jnp.transpose(jnp.broadcast_to(sums, (tile, 128)))[:8]
            else:
                sum_out[to_rows, :] = sums


def add_labels(table, bias, labels, sets, *, step, pieces, parts, part_rows, reps, where="all", out=jnp.float32):
    embed_width = labels[0].shape[1] - sets[0][0].shape[1] if pieces else labels[1].shape[1]
    first, received = len(sets[0]) == 2, len(sets[0]) > 4
    spec = (step, pieces, part_rows, len(sets), first, where, reps, received)
    operands = [bias, *labels]
    aliases, out_shape = {}, []
    for k, one in enumerate(sets):
        docs = one[0]
        rows = {"all": docs.shape[0], "home": docs.shape[0] // reps, "away": docs.shape[0] // reps * (reps - 1)}[where]
        if where == "all" and not first:
            aliases[1 + len(operands) + 2] = 2 * k
            aliases[1 + len(operands) + 3] = 2 * k + 1
        operands += one
        out_shape.append(jax.ShapeDtypeStruct((rows, embed_width), out))
        out_shape.append(jax.ShapeDtypeStruct((rows, 1) if out == jnp.float32 else (8, rows), jnp.float32))
    if pieces and where == "all":
        out_shape.append(jax.ShapeDtypeStruct((8, parts * part_rows), jnp.float32))
    outs = pl.pallas_call(
        functools.partial(accumulate, spec),
        in_specs=[pl.BlockSpec(memory_space=pltpu.SMEM)] + [pl.BlockSpec(memory_space=pltpu.VMEM)] * len(operands),
        out_specs=[pl.BlockSpec(memory_space=pltpu.VMEM)] * len(out_shape),
        out_shape=out_shape,
        input_output_aliases=aliases,
        compiler_params=pltpu.CompilerParams(vmem_limit_bytes=VMEM_LIMIT),
        cost_estimate=pl.CostEstimate(flops=0, bytes_accessed=0, transcendentals=0),
    )(table, *operands)
    totals = [list(outs[2 * k : 2 * k + 2]) for k in range(len(sets))]
    return (totals, outs[-1]) if len(outs) > 2 * len(sets) else totals


def combine(mix_ref, sum_ref, *refs):
    out_ref, others = refs[-1], list(refs[:-1])
    mix, sums = mix_ref[...], sum_ref[...]
    while others:
        parts, rows = [], 0
        while rows < mix.shape[0]:
            parts.append(others.pop(0)[...].astype(jnp.float32))
            rows += parts[-1].shape[0]
        mix = mix + joined(parts, 0)
        sums = sums + column(others.pop(0)[...])
    out_ref[...] = (mix / jnp.sqrt(1.0 + sums)).astype(out_ref.dtype)


def combined(mix, sums, others):
    return pl.pallas_call(
        combine,
        in_specs=[pl.BlockSpec(memory_space=pltpu.VMEM)] * (2 + len(others)),
        out_specs=pl.BlockSpec(memory_space=pltpu.VMEM),
        out_shape=jax.ShapeDtypeStruct(mix.shape, jnp.bfloat16),
        compiler_params=pltpu.CompilerParams(vmem_limit_bytes=VMEM_LIMIT),
        cost_estimate=pl.CostEstimate(flops=0, bytes_accessed=0, transcendentals=0),
    )(mix, sums, *others)


def pack(spec, table, weight, embed, bias, out, sems):
    offset, rows, part_rows, groups = spec
    width = weight.shape[1]
    group = table[0]
    source = pl.ds(pl.multiple_of(group * part_rows + offset, 16), rows)
    copies = [
        pltpu.make_async_copy(weight.at[source, :], out.at[pl.ds(0, rows), pl.ds(0, width)], sems.at[0]),
        pltpu.make_async_copy(embed.at[source, :], out.at[pl.ds(0, rows), pl.ds(width, embed.shape[1])], sems.at[1]),
    ]
    for copy in copies:
        copy.start()
    if offset == 0:
        row = bias[:, :part_rows]
        for other in range(1, groups):
            row = jnp.where(group == other, bias[:, other * part_rows : (other + 1) * part_rows], row)
        out[rows:, :part_rows] = jnp.broadcast_to(row, (BIAS_ROWS, part_rows)).astype(out.dtype)
        out[rows:, part_rows:] = jnp.zeros((BIAS_ROWS, out.shape[1] - part_rows), out.dtype)
    for copy in copies:
        copy.wait()


def packed_part(table, weight, embed, bias, offset, rows, part_rows, groups, cost):
    width = weight.shape[1] + embed.shape[1]
    return pl.pallas_call(
        functools.partial(pack, (offset, rows, part_rows, groups)),
        in_specs=[pl.BlockSpec(memory_space=pltpu.SMEM)]
        + [pl.BlockSpec(memory_space=pl.ANY)] * 2
        + [pl.BlockSpec(memory_space=pltpu.VMEM)],
        out_specs=pl.BlockSpec(memory_space=pltpu.VMEM),
        out_shape=jax.ShapeDtypeStruct((rows + (0 if offset else BIAS_ROWS), width), weight.dtype),
        scratch_shapes=[pltpu.SemaphoreType.DMA((2,))],
        compiler_params=pltpu.CompilerParams(vmem_limit_bytes=VMEM_LIMIT),
        cost_estimate=pl.CostEstimate(flops=cost, bytes_accessed=0, transcendentals=0),
    )(table, *[pltpu.with_memory_space_constraint(x, pltpu.HBM) for x in (weight, embed)], bias)


def per_device(sizes, documents, block_ids, label_weight, label_bias, label_embed):
    groups, loop, reps = sizes
    cores = 2 if loop % 2 == 0 else 1
    chips = loop // cores
    doc_count = documents.shape[0]
    part_rows = label_weight.shape[0] // groups

    def moved(x, to):
        pairs = []
        for g in range(groups):
            for l in range(loop):
                for r in range(reps):
                    g2, z2, c2, r2 = to(g, l // cores, l % cores, r)
                    there = (g2 % groups, (z2 % chips) * cores + c2 % cores, r2 % reps)
                    number = lambda a: (a[0] * loop + a[1]) * reps + a[2]
                    pairs.append((number((g, l, r)), number(there)))
        return lax.ppermute(x, AXES, pairs)

    along = lambda x: moved(x, lambda g, z, c, r: (g, z + 1, c, r))
    across = lambda x, k: moved(x, lambda g, z, c, r: (g + k, z, c, r))
    other_core = lambda x: moved(x, lambda g, z, c, r: (g, z, c + 1, r))
    other_rep = lambda x, k: moved(x, lambda g, z, c, r: (g, z, c, r + k))

    place = lax.axis_index("loop")
    chip, core = place // cores, place % cores
    entries = [lax.axis_index("groups")]
    entries += [((chip - step) % chips) * cores + core for step in range(chips)]
    entries.append(lax.axis_index("rep"))
    table = jnp.stack(entries).astype(jnp.int32)

    total = sum(SHARES)
    cuts = [part_rows * sum(SHARES[:k]) // total // 16 * 16 for k in range(len(SHARES))] + [part_rows]
    chunks = [(a, b - a) for a, b in zip(cuts, cuts[1:])]
    bias = label_bias.astype(jnp.float32)[None, :]
    flying = [
        packed_part(table, label_weight, label_embed, bias, offset, rows, part_rows, groups, COST_NEXT if offset else 0)
        for offset, rows in chunks
    ]
    sets = [[documents, block_ids]]
    if cores == 2:
        sets.append([other_core(documents), other_core(block_ids)])
    call = functools.partial(add_labels, table)
    common = dict(parts=groups, part_rows=part_rows, reps=reps)
    history = [call(bias, [label_weight, label_embed], sets, step=0, pieces=(), **common)]

    def after(x, step, index):
        back = TIES.get(("last" if step + 1 == chips else "first" if step == 1 else "mid", index))
        if back is None or back > step:
            return x
        x, history[step - back] = lax.optimization_barrier((x, history[step - back]))
        return x

    def kernel(pieces, bias, step):
        arrays = [x for _, x in pieces]
        one = [s + t for s, t in zip(sets, history[-1])]
        return call(bias, arrays, one, step=step, pieces=tuple(place for place, _ in pieces), **common)

    final = len(chunks) - 1
    for step in range(1, chips):
        earlier, arrived = (arrived if step > 1 else None), []
        for index, (offset, rows) in enumerate(chunks):
            near = rows * NEAR // 128 // 16 * 16 if step + 1 == chips and index == final and step > 1 else rows
            flying[index] = after(along(flying[index]), step, index)
            pieces = [((0, offset), flying[index])]
            for k in range(1, groups):
                pieces.append(((k, offset), across(flying[index][:near] if near < rows else flying[index], k)))
                if near < rows:
                    pieces.append(((k, offset + near), along(earlier[index][k][1][near:])))
            arrived.append(pieces)
        if step + 1 < chips:
            history.append(kernel(sum(arrived, []), bias, step)[0])
    totals, bias = kernel(sum(arrived[:final], []), bias, chips - 1)
    held = [one + t for one, t in zip(sets, totals)]
    labels = [x for _, x in arrived[final]]
    here = dict(step=chips - 1, pieces=tuple(place for place, _ in arrived[final]), **common)
    call = functools.partial(call, bias)

    narrow = dict(out=jnp.bfloat16, **here)
    tile_docs = doc_count // reps
    others = []
    away = [held[0]]
    if cores == 2:
        (share,) = call(labels, [held[1]], where="away", **narrow)
        away = [held[0] + [other_core(x) for x in share]]
    (away,) = call(labels, away, where="away", **narrow)
    if cores == 2:
        away, held[1] = lax.optimization_barrier((away, held[1]))
        (share,) = call(labels, [held[1]], where="home", **narrow)
        half = tile_docs // 2
        others += [other_core(share[0][:half]), other_core(share[0][half:]), other_core(share[1])]
    ((home_mix, home_sum),) = call(labels, [held[0]], where="home", **here)
    for k in range(1, reps):
        part = slice((k - 1) * tile_docs, k * tile_docs)
        others += [other_rep(away[0][part], k), other_rep(away[1][:, part], k)]
    return combined(home_mix, home_sum, others)


def solution(mesh):
    sizes = tuple(mesh.shape[axis] for axis in AXES)
    return jax.shard_map(
        functools.partial(per_device, sizes),
        mesh=mesh,
        in_specs=(
            P(("groups", "loop"), None),
            P(("groups", "loop"), None),
            P(("loop", "rep"), None),
            P(("loop", "rep")),
            P(("loop", "rep"), None),
        ),
        out_specs=P(("groups", "loop", "rep"), None),
        check_vma=False,
    )
```

```python
import functools

import jax
import jax.numpy as jnp
from jax import lax
from jax.experimental import pallas as pl
from jax.experimental.pallas import tpu as pltpu
from jax.sharding import PartitionSpec as P

AXES = ("groups", "loop", "rep")
DOC_TILE = 1024
VMEM_LIMIT = 24 * 1024 * 1024
SHARES = (1, 1)
TIES = {("first", 0): 1, ("mid", 1): 1, ("last", 1): 1}
BIAS_ROWS = 8
NEAR = 64
HALVES = 2
COST_PIECE = 8100000000
COST_NEXT = 13200000000


def joined(xs, axis):
    return xs[0] if len(xs) == 1 else jnp.concatenate(xs, axis=axis)


def column(row):
    return jnp.transpose(jnp.broadcast_to(row[:1], (128, row.shape[1])))[:, :1]


def accumulate(spec, table, bias_ref, *refs):
    step, pieces, part_rows, sets, first, where, reps, received, narrow = spec
    count = max(2, len(pieces))
    labels, refs = refs[:count], refs[count:]
    if pieces:
        width = refs[0].shape[1]
        leads = {part: ref for (part, offset), ref in zip(pieces, labels) if offset == 0}
        bias_rows, weight_rows, embed_rows = [], [], []
        for (part, offset), ref in zip(pieces, labels):
            rows = ref.shape[0] - (0 if offset else BIAS_ROWS)
            weight_rows.append(ref[:rows, :width])
            embed_rows.append(ref[:rows, width:])
            if leads:
                lead = leads[part]
                row = lead[lead.shape[0] - BIAS_ROWS :, :part_rows].astype(jnp.float32)[:1]
            else:
                row = bias_ref[:1, part * part_rows : (part + 1) * part_rows]
            if where[0] == "all" and offset == 0:
                refs[-1][:, part * part_rows : (part + 1) * part_rows] = jnp.broadcast_to(row, (8, part_rows))
            bias_rows.append(row[:, offset : offset + rows])
        bias = joined(bias_rows, 1)
        weight_rows, embed_rows = joined(weight_rows, 0), joined(embed_rows, 0)
    else:
        weight_rows, embed_rows, bias = labels[0][...], labels[1][...], bias_ref[...]
    block, rep = table[1 + step], table[table.shape[0] - 1]
    per_set = 2 + (0 if first else 2) + (1 if received else 0)
    kind, piece, count = where
    outs = refs[sets * per_set :]
    for k in range(sets):
        docs_ref, ids_ref, *rest = refs[k * per_set : (k + 1) * per_set]
        held = docs_ref.shape[0] // (1 if kind == "all" else reps)
        tile = min(DOC_TILE, held) if kind == "all" else held // count
        mix_out = outs[k if narrow else 2 * k]
        spare = sum_rows(reps)
        stride = tile + spare

        @pl.loop(0, {"all": held // tile, "home": 1, "away": reps - 1}[kind])
        def _(i):
            if kind == "all":
                start = i * tile
            elif kind == "home":
                start = rep * held + piece * tile
            else:
                start = lax.rem(rep + 1 + i, reps) * held + piece * tile
            from_rows = pl.ds(pl.multiple_of(start, tile), tile)
            chosen = jnp.max((ids_ref[from_rows, :] == block).astype(jnp.float32), axis=1, keepdims=True)
            logits = lax.dot_general(
                docs_ref[from_rows, :], weight_rows, (((1,), (1,)), ((), ())), preferred_element_type=jnp.float32
            )
            weights = (chosen * jax.nn.sigmoid(logits + bias)).astype(jnp.bfloat16)
            mix = jnp.dot(weights, embed_rows, preferred_element_type=jnp.float32)
            sums = jnp.sum(weights.astype(jnp.float32), axis=1, keepdims=True)
            if not first:
                mix = mix + rest[0][from_rows, :]
                sums = sums + rest[1][from_rows, :]
            at = pl.multiple_of(i * stride, spare)
            if received:
                mix = mix + rest[2][pl.ds(at, tile), :].astype(jnp.float32)
                sums = sums + sums_from(rest[2][pl.ds(at + tile, spare), :], tile)
            if narrow:
                mix_out[pl.ds(at, tile), :] = mix.astype(mix_out.dtype)
                mix_out[pl.ds(at + tile, spare), :] = sums_to(sums, spare, mix_out.shape[1]).astype(mix_out.dtype)
            else:
                to_rows = pl.ds(pl.multiple_of(i * tile, tile), tile)
                mix_out[to_rows, :] = mix
                outs[2 * k + 1][to_rows, :] = sums


def sum_rows(reps):
    return 8 if reps == 2 else 16


def sums_to(sums, spare, width):
    rows = jnp.transpose(jnp.broadcast_to(sums, (sums.shape[0], 128)))[:spare]
    high = rows.astype(jnp.bfloat16).astype(jnp.float32)
    place = lax.broadcasted_iota(jnp.int32, rows.shape, 0)
    rows = jnp.where(place == 0, high, jnp.where(place == 1, rows - high, 0.0))
    if rows.shape[1] == width:
        return rows
    return jnp.concatenate([rows, jnp.zeros((spare, width - rows.shape[1]), jnp.float32)], axis=1)


def sums_from(rows, count):
    rows = rows.astype(jnp.float32)[:, :count]
    return column(rows[:1] + rows[1:2])


def add_labels(table, bias, labels, sets, *, step, pieces, parts, part_rows, reps, where=("all", 0, 1), narrow=False):
    embed_width = labels[0].shape[1] - sets[0][0].shape[1] if pieces else labels[1].shape[1]
    first, received = len(sets[0]) == 2, len(sets[0]) > 4
    spec = (step, pieces, part_rows, len(sets), first, where, reps, received, narrow)
    operands = [bias, *labels]
    aliases, out_shape = {}, []
    kind, _, count = where
    for k, one in enumerate(sets):
        held = one[0].shape[0] // (1 if kind == "all" else reps)
        if kind == "all" and not first:
            aliases[1 + len(operands) + 2] = 2 * k
            aliases[1 + len(operands) + 3] = 2 * k + 1
        operands += one
        if narrow:
            rows = (held // count + sum_rows(reps)) * (reps - 1 if kind == "away" else 1)
            out_shape.append(jax.ShapeDtypeStruct((rows, embed_width), jnp.bfloat16))
        else:
            out_shape.append(jax.ShapeDtypeStruct((held, embed_width), jnp.float32))
            out_shape.append(jax.ShapeDtypeStruct((held, 1), jnp.float32))
    if pieces and kind == "all":
        out_shape.append(jax.ShapeDtypeStruct((8, parts * part_rows), jnp.float32))
    outs = pl.pallas_call(
        functools.partial(accumulate, spec),
        in_specs=[pl.BlockSpec(memory_space=pltpu.SMEM)] + [pl.BlockSpec(memory_space=pltpu.VMEM)] * len(operands),
        out_specs=[pl.BlockSpec(memory_space=pltpu.VMEM)] * len(out_shape),
        out_shape=out_shape,
        input_output_aliases=aliases,
        compiler_params=pltpu.CompilerParams(vmem_limit_bytes=VMEM_LIMIT),
        cost_estimate=pl.CostEstimate(flops=0, bytes_accessed=0, transcendentals=0),
    )(table, *operands)
    if narrow:
        return outs[0]
    totals = [list(outs[2 * k : 2 * k + 2]) for k in range(len(sets))]
    return (totals, outs[-1]) if len(outs) > 2 * len(sets) else totals


def combine(spec, mix_ref, sum_ref, *refs):
    piece, count, shares = spec
    out_ref, held, sem = refs[-3:]
    rows = mix_ref.shape[0] // count
    where = slice(piece * rows, (piece + 1) * rows)
    mix, sums = mix_ref[where, :], sum_ref[where, :]
    for arrays in shares:
        parts, refs = refs[:arrays], refs[arrays:]
        left = rows - sum(ref.shape[0] for ref in parts[:-1])
        mix = mix + joined([ref[...].astype(jnp.float32) for ref in parts[:-1]] + [parts[-1][:left, :].astype(jnp.float32)], 0)
        sums = sums + sums_from(parts[-1][left:, :], rows)
    held[...] = (mix / jnp.sqrt(1.0 + sums)).astype(held.dtype)
    copy = pltpu.make_async_copy(held, out_ref.at[pl.ds(piece * rows, rows), :], sem)
    copy.start()
    copy.wait()


def combined(mix, sums, shares):
    count, out = len(shares), None
    for piece in range(count):
        operands = [mix, sums, *sum(shares[piece], [])]
        in_specs = [pl.BlockSpec(memory_space=pltpu.VMEM)] * len(operands)
        aliases = {}
        if out is not None:
            operands.append(out)
            in_specs.append(pl.BlockSpec(memory_space=pl.ANY))
            aliases = {len(operands) - 1: 0}
        out = pl.pallas_call(
            functools.partial(combine, (piece, count, tuple(len(arrays) for arrays in shares[piece]))),
            in_specs=in_specs,
            out_specs=pl.BlockSpec(memory_space=pl.ANY),
            out_shape=jax.ShapeDtypeStruct(mix.shape, jnp.bfloat16),
            input_output_aliases=aliases,
            scratch_shapes=[pltpu.VMEM((mix.shape[0] // count, mix.shape[1]), jnp.bfloat16), pltpu.SemaphoreType.DMA(())],
            compiler_params=pltpu.CompilerParams(vmem_limit_bytes=VMEM_LIMIT),
            cost_estimate=pl.CostEstimate(flops=COST_PIECE, bytes_accessed=0, transcendentals=0),
        )(*operands)
    return out


def pack(spec, table, weight, embed, bias, out, sems):
    offset, rows, part_rows, groups = spec
    width = weight.shape[1]
    group = table[0]
    source = pl.ds(pl.multiple_of(group * part_rows + offset, 16), rows)
    copies = [
        pltpu.make_async_copy(weight.at[source, :], out.at[pl.ds(0, rows), pl.ds(0, width)], sems.at[0]),
        pltpu.make_async_copy(embed.at[source, :], out.at[pl.ds(0, rows), pl.ds(width, embed.shape[1])], sems.at[1]),
    ]
    for copy in copies:
        copy.start()
    if offset == 0:
        row = bias[:, :part_rows]
        for other in range(1, groups):
            row = jnp.where(group == other, bias[:, other * part_rows : (other + 1) * part_rows], row)
        out[rows:, :part_rows] = jnp.broadcast_to(row, (BIAS_ROWS, part_rows)).astype(out.dtype)
        out[rows:, part_rows:] = jnp.zeros((BIAS_ROWS, out.shape[1] - part_rows), out.dtype)
    for copy in copies:
        copy.wait()


def packed_part(table, weight, embed, bias, offset, rows, part_rows, groups, cost):
    width = weight.shape[1] + embed.shape[1]
    return pl.pallas_call(
        functools.partial(pack, (offset, rows, part_rows, groups)),
        in_specs=[pl.BlockSpec(memory_space=pltpu.SMEM)]
        + [pl.BlockSpec(memory_space=pl.ANY)] * 2
        + [pl.BlockSpec(memory_space=pltpu.VMEM)],
        out_specs=pl.BlockSpec(memory_space=pltpu.VMEM),
        out_shape=jax.ShapeDtypeStruct((rows + (0 if offset else BIAS_ROWS), width), weight.dtype),
        scratch_shapes=[pltpu.SemaphoreType.DMA((2,))],
        compiler_params=pltpu.CompilerParams(vmem_limit_bytes=VMEM_LIMIT),
        cost_estimate=pl.CostEstimate(flops=cost, bytes_accessed=0, transcendentals=0),
    )(table, *[pltpu.with_memory_space_constraint(x, pltpu.HBM) for x in (weight, embed)], bias)


def per_device(sizes, documents, block_ids, label_weight, label_bias, label_embed):
    groups, loop, reps = sizes
    cores = 2 if loop % 2 == 0 else 1
    chips = loop // cores
    doc_count = documents.shape[0]
    part_rows = label_weight.shape[0] // groups

    def moved(x, to):
        pairs = []
        for g in range(groups):
            for l in range(loop):
                for r in range(reps):
                    g2, z2, c2, r2 = to(g, l // cores, l % cores, r)
                    there = (g2 % groups, (z2 % chips) * cores + c2 % cores, r2 % reps)
                    number = lambda a: (a[0] * loop + a[1]) * reps + a[2]
                    pairs.append((number((g, l, r)), number(there)))
        return lax.ppermute(x, AXES, pairs)

    along = lambda x: moved(x, lambda g, z, c, r: (g, z + 1, c, r))
    across = lambda x, k: moved(x, lambda g, z, c, r: (g + k, z, c, r))
    other_core = lambda x: moved(x, lambda g, z, c, r: (g, z, c + 1, r))
    other_rep = lambda x, k: moved(x, lambda g, z, c, r: (g, z, c, r + k))

    place = lax.axis_index("loop")
    chip, core = place // cores, place % cores
    entries = [lax.axis_index("groups")]
    entries += [((chip - step) % chips) * cores + core for step in range(chips)]
    entries.append(lax.axis_index("rep"))
    table = jnp.stack(entries).astype(jnp.int32)

    total = sum(SHARES)
    cuts = [part_rows * sum(SHARES[:k]) // total // 16 * 16 for k in range(len(SHARES))] + [part_rows]
    chunks = [(a, b - a) for a, b in zip(cuts, cuts[1:])]
    bias = label_bias.astype(jnp.float32)[None, :]
    flying = [
        packed_part(table, label_weight, label_embed, bias, offset, rows, part_rows, groups, COST_NEXT if offset else 0)
        for offset, rows in chunks
    ]
    sets = [[documents, block_ids]]
    if cores == 2:
        sets.append([other_core(documents), other_core(block_ids)])
    call = functools.partial(add_labels, table)
    common = dict(parts=groups, part_rows=part_rows, reps=reps)
    history = [call(bias, [label_weight, label_embed], sets, step=0, pieces=(), **common)]

    def after(x, step, index):
        back = TIES.get(("last" if step + 1 == chips else "first" if step == 1 else "mid", index))
        if back is None or back > step:
            return x
        x, history[step - back] = lax.optimization_barrier((x, history[step - back]))
        return x

    def kernel(pieces, bias, step):
        arrays = [x for _, x in pieces]
        one = [s + t for s, t in zip(sets, history[-1])]
        return call(bias, arrays, one, step=step, pieces=tuple(place for place, _ in pieces), **common)

    final = len(chunks) - 1
    for step in range(1, chips):
        earlier, arrived = (arrived if step > 1 else None), []
        for index, (offset, rows) in enumerate(chunks):
            near = rows * NEAR // 128 // 16 * 16 if step + 1 == chips and index == final and step > 1 else rows
            flying[index] = after(along(flying[index]), step, index)
            pieces = [((0, offset), flying[index])]
            for k in range(1, groups):
                pieces.append(((k, offset), across(flying[index][:near] if near < rows else flying[index], k)))
                if near < rows:
                    pieces.append(((k, offset + near), along(earlier[index][k][1][near:])))
            arrived.append(pieces)
        if step + 1 < chips:
            history.append(kernel(sum(arrived, []), bias, step)[0])
    totals, bias = kernel(sum(arrived[:final], []), bias, chips - 1)
    held = [one + t for one, t in zip(sets, totals)]
    labels = [x for _, x in arrived[final]]
    here = dict(step=chips - 1, pieces=tuple(place for place, _ in arrived[final]), **common)
    call = functools.partial(call, bias)

    tile_docs = doc_count // reps
    halves = HALVES if tile_docs // HALVES >= 128 else 1
    given = [None] * halves
    if cores == 2:
        for h in range(halves):
            given[h] = other_core(call(labels, [held[1]], where=("away", h, halves), narrow=True, **here))
    shares = []
    for h in range(halves):
        one = held[0] + ([given[h]] if cores == 2 else [])
        share = call(labels, [one], where=("away", h, halves), narrow=True, **here)
        stride = share.shape[0] // (reps - 1)
        if h == 0:
            lead = share
        shares.append([[other_rep(share if reps == 2 else share[k * stride - stride : k * stride], k)] for k in range(1, reps)])
    if cores == 2:
        lead, held[1] = lax.optimization_barrier((lead, held[1]))
        for h in range(halves):
            share = call(labels, [held[1]], where=("home", h, halves), narrow=True, **here)
            cut = tile_docs // halves // 2
            shares[h].append([other_core(share[:cut]), other_core(share[cut:])])
    ((home_mix, home_sum),) = call(labels, [held[0]], where=("home", 0, 1), **here)
    return combined(home_mix, home_sum, shares)


def solution(mesh):
    sizes = tuple(mesh.shape[axis] for axis in AXES)
    return jax.shard_map(
        functools.partial(per_device, sizes),
        mesh=mesh,
        in_specs=(
            P(("groups", "loop"), None),
            P(("groups", "loop"), None),
            P(("loop", "rep"), None),
            P(("loop", "rep")),
            P(("loop", "rep"), None),
        ),
        out_specs=P(("groups", "loop", "rep"), None),
        check_vma=False,
    )
```

```python
import functools

import jax
import jax.numpy as jnp
from jax import lax
from jax.experimental import pallas as pl
from jax.experimental.pallas import tpu as pltpu
from jax.sharding import PartitionSpec as P

AXES = ("groups", "loop", "rep")
DOC_TILE = 1024
VMEM_LIMIT = 24 * 1024 * 1024
SHARES = (1, 1)
TIES = {("first", 0): 1, ("mid", 1): 1, ("last", 1): 1}
BIAS_ROWS = 8
NEAR = 64
HALVES = 2
COST_PIECE = 8100000000
COST_NEXT = 13200000000


def joined(xs, axis):
    return xs[0] if len(xs) == 1 else jnp.concatenate(xs, axis=axis)


def column(row):
    return jnp.transpose(jnp.broadcast_to(row[:1], (128, row.shape[1])))[:, :1]


def accumulate(spec, table, bias_ref, *refs):
    step, pieces, part_rows, sets, first, where, reps, received, narrow = spec
    count = max(2, len(pieces))
    labels, refs = refs[:count], refs[count:]
    if pieces:
        width = refs[0].shape[1]
        leads = {part: ref for (part, offset), ref in zip(pieces, labels) if offset == 0}
        bias_rows, weight_rows, embed_rows = [], [], []
        for (part, offset), ref in zip(pieces, labels):
            rows = ref.shape[0] - (0 if offset else BIAS_ROWS)
            weight_rows.append(ref[:rows, :width])
            embed_rows.append(ref[:rows, width:])
            if leads:
                lead = leads[part]
                row = lead[lead.shape[0] - BIAS_ROWS :, :part_rows].astype(jnp.float32)[:1]
            else:
                row = bias_ref[:1, part * part_rows : (part + 1) * part_rows]
            if where[0] == "all" and offset == 0:
                refs[-1][:, part * part_rows : (part + 1) * part_rows] = jnp.broadcast_to(row, (8, part_rows))
            bias_rows.append(row[:, offset : offset + rows])
        bias = joined(bias_rows, 1)
        weight_rows, embed_rows = joined(weight_rows, 0), joined(embed_rows, 0)
    else:
        weight_rows, embed_rows, bias = labels[0][...], labels[1][...], bias_ref[...].astype(jnp.float32)
    block, rep = table[1 + step], table[table.shape[0] - 1]
    per_set = 2 + (0 if first else 2) + (1 if received else 0)
    kind, piece, count = where
    outs = refs[sets * per_set :]
    for k in range(sets):
        docs_ref, ids_ref, *rest = refs[k * per_set : (k + 1) * per_set]
        held = docs_ref.shape[0] // (1 if kind == "all" else reps)
        tile = min(DOC_TILE, held) if kind == "all" else held // count
        mix_out = outs[k if narrow else 2 * k]
        spare = sum_rows(reps)
        stride = tile + spare

        @pl.loop(0, {"all": held // tile, "home": 1, "away": reps - 1}[kind])
        def _(i):
            if kind == "all":
                start = i * tile
            elif kind == "home":
                start = rep * held + piece * tile
            else:
                start = lax.rem(rep + 1 + i, reps) * held + piece * tile
            from_rows = pl.ds(pl.multiple_of(start, tile), tile)
            chosen = jnp.max((ids_ref[from_rows, :] == block).astype(jnp.float32), axis=1, keepdims=True)
            logits = lax.dot_general(
                docs_ref[from_rows, :], weight_rows, (((1,), (1,)), ((), ())), preferred_element_type=jnp.float32
            )
            weights = (chosen * jax.nn.sigmoid(logits + bias)).astype(jnp.bfloat16)
            mix = jnp.dot(weights, embed_rows, preferred_element_type=jnp.float32)
            sums = jnp.sum(weights.astype(jnp.float32), axis=1, keepdims=True)
            if not first:
                mix = mix + rest[0][from_rows, :]
                sums = sums + rest[1][from_rows, :]
            at = pl.multiple_of(i * stride, spare)
            if received:
                mix = mix + rest[2][pl.ds(at, tile), :].astype(jnp.float32)
                sums = sums + sums_from(rest[2][pl.ds(at + tile, spare), :], tile)
            if narrow:
                mix_out[pl.ds(at, tile), :] = mix.astype(mix_out.dtype)
                mix_out[pl.ds(at + tile, spare), :] = sums_to(sums, spare, mix_out.shape[1]).astype(mix_out.dtype)
            else:
                to_rows = pl.ds(pl.multiple_of(i * tile, tile), tile)
                mix_out[to_rows, :] = mix
                outs[2 * k + 1][to_rows, :] = sums


def sum_rows(reps):
    return 8 if reps == 2 else 16


def sums_to(sums, spare, width):
    rows = jnp.transpose(jnp.broadcast_to(sums, (sums.shape[0], 128)))[:spare]
    high = rows.astype(jnp.bfloat16).astype(jnp.float32)
    place = lax.broadcasted_iota(jnp.int32, rows.shape, 0)
    rows = jnp.where(place == 0, high, jnp.where(place == 1, rows - high, 0.0))
    if rows.shape[1] == width:
        return rows
    return jnp.concatenate([rows, jnp.zeros((spare, width - rows.shape[1]), jnp.float32)], axis=1)


def sums_from(rows, count):
    rows = rows.astype(jnp.float32)[:, :count]
    return column(rows[:1] + rows[1:2])


def add_labels(table, bias, labels, sets, *, step, pieces, parts, part_rows, reps, where=("all", 0, 1), narrow=False):
    embed_width = labels[0].shape[1] - sets[0][0].shape[1] if pieces else labels[1].shape[1]
    first, received = len(sets[0]) == 2, len(sets[0]) > 4
    spec = (step, pieces, part_rows, len(sets), first, where, reps, received, narrow)
    operands = [bias, *labels]
    aliases, out_shape = {}, []
    kind, _, count = where
    for k, one in enumerate(sets):
        held = one[0].shape[0] // (1 if kind == "all" else reps)
        if kind == "all" and not first:
            aliases[1 + len(operands) + 2] = 2 * k
            aliases[1 + len(operands) + 3] = 2 * k + 1
        operands += one
        if narrow:
            rows = (held // count + sum_rows(reps)) * (reps - 1 if kind == "away" else 1)
            out_shape.append(jax.ShapeDtypeStruct((rows, embed_width), jnp.bfloat16))
        else:
            out_shape.append(jax.ShapeDtypeStruct((held, embed_width), jnp.float32))
            out_shape.append(jax.ShapeDtypeStruct((held, 1), jnp.float32))
    if pieces and kind == "all":
        out_shape.append(jax.ShapeDtypeStruct((8, parts * part_rows), jnp.float32))
    outs = pl.pallas_call(
        functools.partial(accumulate, spec),
        in_specs=[pl.BlockSpec(memory_space=pltpu.SMEM)] + [pl.BlockSpec(memory_space=pltpu.VMEM)] * len(operands),
        out_specs=[pl.BlockSpec(memory_space=pltpu.VMEM)] * len(out_shape),
        out_shape=out_shape,
        input_output_aliases=aliases,
        compiler_params=pltpu.CompilerParams(vmem_limit_bytes=VMEM_LIMIT),
        cost_estimate=pl.CostEstimate(flops=0, bytes_accessed=0, transcendentals=0),
    )(table, *operands)
    if narrow:
        return outs[0]
    totals = [list(outs[2 * k : 2 * k + 2]) for k in range(len(sets))]
    return (totals, outs[-1]) if len(outs) > 2 * len(sets) else totals


def combine(spec, mix_ref, sum_ref, *refs):
    piece, count, shares = spec
    out_ref, held, sem = refs[-3:]
    rows = mix_ref.shape[0] // count
    where = slice(piece * rows, (piece + 1) * rows)
    mix, sums = mix_ref[where, :], sum_ref[where, :]
    for arrays in shares:
        parts, refs = refs[:arrays], refs[arrays:]
        left = rows - sum(ref.shape[0] for ref in parts[:-1])
        mix = mix + joined([ref[...].astype(jnp.float32) for ref in parts[:-1]] + [parts[-1][:left, :].astype(jnp.float32)], 0)
        sums = sums + sums_from(parts[-1][left:, :], rows)
    held[...] = (mix / jnp.sqrt(1.0 + sums)).astype(held.dtype)
    copy = pltpu.make_async_copy(held, out_ref.at[pl.ds(piece * rows, rows), :], sem)
    copy.start()
    copy.wait()


def combined(mix, sums, shares):
    count, out = len(shares), None
    for piece in range(count):
        operands = [mix, sums, *sum(shares[piece], [])]
        in_specs = [pl.BlockSpec(memory_space=pltpu.VMEM)] * len(operands)
        aliases = {}
        if out is not None:
            operands.append(out)
            in_specs.append(pl.BlockSpec(memory_space=pl.ANY))
            aliases = {len(operands) - 1: 0}
        out = pl.pallas_call(
            functools.partial(combine, (piece, count, tuple(len(arrays) for arrays in shares[piece]))),
            in_specs=in_specs,
            out_specs=pl.BlockSpec(memory_space=pl.ANY),
            out_shape=jax.ShapeDtypeStruct(mix.shape, jnp.bfloat16),
            input_output_aliases=aliases,
            scratch_shapes=[pltpu.VMEM((mix.shape[0] // count, mix.shape[1]), jnp.bfloat16), pltpu.SemaphoreType.DMA(())],
            compiler_params=pltpu.CompilerParams(vmem_limit_bytes=VMEM_LIMIT),
            cost_estimate=pl.CostEstimate(flops=COST_PIECE, bytes_accessed=0, transcendentals=0),
        )(*operands)
    return out


def pack(spec, table, weight, embed, bias, out, sems):
    offset, rows, part_rows, groups = spec
    width = weight.shape[1]
    group = table[0]
    source = pl.ds(pl.multiple_of(group * part_rows + offset, 16), rows)
    copies = [
        pltpu.make_async_copy(weight.at[source, :], out.at[pl.ds(0, rows), pl.ds(0, width)], sems.at[0]),
        pltpu.make_async_copy(embed.at[source, :], out.at[pl.ds(0, rows), pl.ds(width, embed.shape[1])], sems.at[1]),
    ]
    for copy in copies:
        copy.start()
    if offset == 0:
        every = bias[...].astype(jnp.float32)
        row = every[:, :part_rows]
        for other in range(1, groups):
            row = jnp.where(group == other, every[:, other * part_rows : (other + 1) * part_rows], row)
        out[rows:, :part_rows] = jnp.broadcast_to(row, (BIAS_ROWS, part_rows)).astype(out.dtype)
        out[rows:, part_rows:] = jnp.zeros((BIAS_ROWS, out.shape[1] - part_rows), out.dtype)
    for copy in copies:
        copy.wait()


def packed_part(table, weight, embed, bias, offset, rows, part_rows, groups, cost):
    width = weight.shape[1] + embed.shape[1]
    return pl.pallas_call(
        functools.partial(pack, (offset, rows, part_rows, groups)),
        in_specs=[pl.BlockSpec(memory_space=pltpu.SMEM)]
        + [pl.BlockSpec(memory_space=pl.ANY)] * 2
        + [pl.BlockSpec(memory_space=pltpu.VMEM)],
        out_specs=pl.BlockSpec(memory_space=pltpu.VMEM),
        out_shape=jax.ShapeDtypeStruct((rows + (0 if offset else BIAS_ROWS), width), weight.dtype),
        scratch_shapes=[pltpu.SemaphoreType.DMA((2,))],
        compiler_params=pltpu.CompilerParams(vmem_limit_bytes=VMEM_LIMIT),
        cost_estimate=pl.CostEstimate(flops=cost, bytes_accessed=0, transcendentals=0),
    )(table, *[pltpu.with_memory_space_constraint(x, pltpu.HBM) for x in (weight, embed)], bias)


def per_device(sizes, documents, block_ids, label_weight, label_bias, label_embed):
    groups, loop, reps = sizes
    cores = 2 if loop % 2 == 0 else 1
    chips = loop // cores
    doc_count = documents.shape[0]
    part_rows = label_weight.shape[0] // groups

    def moved(x, to):
        pairs = []
        for g in range(groups):
            for l in range(loop):
                for r in range(reps):
                    g2, z2, c2, r2 = to(g, l // cores, l % cores, r)
                    there = (g2 % groups, (z2 % chips) * cores + c2 % cores, r2 % reps)
                    number = lambda a: (a[0] * loop + a[1]) * reps + a[2]
                    pairs.append((number((g, l, r)), number(there)))
        return lax.ppermute(x, AXES, pairs)

    along = lambda x: moved(x, lambda g, z, c, r: (g, z + 1, c, r))
    across = lambda x, k: moved(x, lambda g, z, c, r: (g + k, z, c, r))
    other_core = lambda x: moved(x, lambda g, z, c, r: (g, z, c + 1, r))
    other_rep = lambda x, k: moved(x, lambda g, z, c, r: (g, z, c, r + k))

    place = lax.axis_index("loop")
    chip, core = place // cores, place % cores
    entries = [lax.axis_index("groups")]
    entries += [((chip - step) % chips) * cores + core for step in range(chips)]
    entries.append(lax.axis_index("rep"))
    table = jnp.stack(entries).astype(jnp.int32)

    total = sum(SHARES)
    cuts = [part_rows * sum(SHARES[:k]) // total // 16 * 16 for k in range(len(SHARES))] + [part_rows]
    chunks = [(a, b - a) for a, b in zip(cuts, cuts[1:])]
    bias = label_bias[None, :]
    sets = [[documents, block_ids]]
    later = table
    if cores == 2:
        sets.append([other_core(documents), other_core(block_ids)])
        later, sets[1][1] = lax.optimization_barrier((table, sets[1][1]))
    flying = [
        packed_part(
            later if offset else table,
            label_weight,
            label_embed,
            bias,
            offset,
            rows,
            part_rows,
            groups,
            COST_NEXT if offset else 0,
        )
        for offset, rows in chunks
    ]
    call = functools.partial(add_labels, table)
    common = dict(parts=groups, part_rows=part_rows, reps=reps)
    history = [call(bias, [label_weight, label_embed], sets, step=0, pieces=(), **common)]

    def after(x, step, index):
        back = TIES.get(("last" if step + 1 == chips else "first" if step == 1 else "mid", index))
        if back is None or back > step:
            return x
        x, history[step - back] = lax.optimization_barrier((x, history[step - back]))
        return x

    def kernel(pieces, bias, step):
        arrays = [x for _, x in pieces]
        one = [s + t for s, t in zip(sets, history[-1])]
        return call(bias, arrays, one, step=step, pieces=tuple(place for place, _ in pieces), **common)

    final = len(chunks) - 1
    for step in range(1, chips):
        earlier, arrived = (arrived if step > 1 else None), []
        for index, (offset, rows) in enumerate(chunks):
            near = rows * NEAR // 128 // 16 * 16 if step + 1 == chips and index == final and step > 1 else rows
            flying[index] = after(along(flying[index]), step, index)
            pieces = [((0, offset), flying[index])]
            for k in range(1, groups):
                pieces.append(((k, offset), across(flying[index][:near] if near < rows else flying[index], k)))
                if near < rows:
                    pieces.append(((k, offset + near), along(earlier[index][k][1][near:])))
            arrived.append(pieces)
        if step + 1 < chips:
            history.append(kernel(sum(arrived, []), bias, step)[0])
    totals, bias = kernel(sum(arrived[:final], []), bias, chips - 1)
    held = [one + t for one, t in zip(sets, totals)]
    labels = [x for _, x in arrived[final]]
    here = dict(step=chips - 1, pieces=tuple(place for place, _ in arrived[final]), **common)
    call = functools.partial(call, bias)

    tile_docs = doc_count // reps
    halves = HALVES if tile_docs // HALVES >= 128 else 1
    given = [None] * halves
    if cores == 2:
        for h in range(halves):
            given[h] = other_core(call(labels, [held[1]], where=("away", h, halves), narrow=True, **here))
    shares = []
    for h in range(halves):
        one = held[0] + ([given[h]] if cores == 2 else [])
        share = call(labels, [one], where=("away", h, halves), narrow=True, **here)
        stride = share.shape[0] // (reps - 1)
        if h == 0:
            lead = share
        shares.append([[other_rep(share if reps == 2 else share[k * stride - stride : k * stride], k)] for k in range(1, reps)])
    if cores == 2:
        lead, held[1] = lax.optimization_barrier((lead, held[1]))
        for h in range(halves):
            share = call(labels, [held[1]], where=("home", h, halves), narrow=True, **here)
            cut = tile_docs // halves // 2
            shares[h].append([other_core(share[:cut]), other_core(share[cut:])])
    ((home_mix, home_sum),) = call(labels, [held[0]], where=("home", 0, 1), **here)
    return combined(home_mix, home_sum, shares)


def solution(mesh):
    sizes = tuple(mesh.shape[axis] for axis in AXES)
    return jax.shard_map(
        functools.partial(per_device, sizes),
        mesh=mesh,
        in_specs=(
            P(("groups", "loop"), None),
            P(("groups", "loop"), None),
            P(("loop", "rep"), None),
            P(("loop", "rep")),
            P(("loop", "rep"), None),
        ),
        out_specs=P(("groups", "loop", "rep"), None),
        check_vma=False,
    )
```

```python
import functools

import jax
import jax.numpy as jnp
from jax import lax
from jax.experimental import pallas as pl
from jax.experimental.pallas import tpu as pltpu
from jax.sharding import PartitionSpec as P

AXES = ("groups", "loop", "rep")
DOC_TILE = 1024
VMEM_LIMIT = 24 * 1024 * 1024
SHARES = (1, 1)
TIES = {("first", 0): 1, ("mid", 1): 1, ("last", 1): 1}
BIAS_ROWS = 8
NEAR = 64
HALVES = 2
COST_PIECE = 8100000000
COST_NEXT = 13200000000


def joined(xs, axis):
    return xs[0] if len(xs) == 1 else jnp.concatenate(xs, axis=axis)


def in_one_row(ref):
    rows = ref[...].astype(jnp.float32)
    return joined([rows[k : k + 1, :] for k in range(rows.shape[0])], 1)


def column(row):
    return jnp.transpose(jnp.broadcast_to(row[:1], (128, row.shape[1])))[:, :1]


def accumulate(spec, table, bias_ref, *refs):
    step, pieces, part_rows, sets, first, where, reps, received, narrow = spec
    count = max(2, len(pieces))
    labels, refs = refs[:count], refs[count:]
    if pieces:
        width = refs[0].shape[1]
        leads = {part: ref for (part, offset), ref in zip(pieces, labels) if offset == 0}
        bias_rows, weight_rows, embed_rows = [], [], []
        for (part, offset), ref in zip(pieces, labels):
            rows = ref.shape[0] - (0 if offset else BIAS_ROWS)
            weight_rows.append(ref[:rows, :width])
            embed_rows.append(ref[:rows, width:])
            if leads:
                lead = leads[part]
                row = lead[lead.shape[0] - BIAS_ROWS :, :part_rows].astype(jnp.float32)[:1]
            else:
                row = bias_ref[:1, part * part_rows : (part + 1) * part_rows]
            if where[0] == "all" and offset == 0:
                refs[-1][:, part * part_rows : (part + 1) * part_rows] = jnp.broadcast_to(row, (8, part_rows))
            bias_rows.append(row[:, offset : offset + rows])
        bias = joined(bias_rows, 1)
        weight_rows, embed_rows = joined(weight_rows, 0), joined(embed_rows, 0)
    else:
        weight_rows, embed_rows, bias = labels[0][...], labels[1][...], in_one_row(bias_ref)
    block, rep = table[1 + step], table[table.shape[0] - 1]
    per_set = 2 + (0 if first else 2) + (1 if received else 0)
    kind, piece, count = where
    outs = refs[sets * per_set :]
    for k in range(sets):
        docs_ref, ids_ref, *rest = refs[k * per_set : (k + 1) * per_set]
        held = docs_ref.shape[0] // (1 if kind == "all" else reps)
        tile = min(DOC_TILE, held) if kind == "all" else held // count
        mix_out = outs[k if narrow else 2 * k]
        spare = sum_rows(reps)
        stride = tile + spare

        @pl.loop(0, {"all": held // tile, "home": 1, "away": reps - 1}[kind])
        def _(i):
            if kind == "all":
                start = i * tile
            elif kind == "home":
                start = rep * held + piece * tile
            else:
                start = lax.rem(rep + 1 + i, reps) * held + piece * tile
            from_rows = pl.ds(pl.multiple_of(start, tile), tile)
            chosen = jnp.max((ids_ref[from_rows, :] == block).astype(jnp.float32), axis=1, keepdims=True)
            logits = lax.dot_general(
                docs_ref[from_rows, :], weight_rows, (((1,), (1,)), ((), ())), preferred_element_type=jnp.float32
            )
            weights = (chosen * jax.nn.sigmoid(logits + bias)).astype(jnp.bfloat16)
            mix = jnp.dot(weights, embed_rows, preferred_element_type=jnp.float32)
            sums = jnp.sum(weights.astype(jnp.float32), axis=1, keepdims=True)
            if not first:
                mix = mix + rest[0][from_rows, :]
                sums = sums + rest[1][from_rows, :]
            at = pl.multiple_of(i * stride, spare)
            if received:
                mix = mix + rest[2][pl.ds(at, tile), :].astype(jnp.float32)
                sums = sums + sums_from(rest[2][pl.ds(at + tile, spare), :], tile)
            if narrow:
                mix_out[pl.ds(at, tile), :] = mix.astype(mix_out.dtype)
                mix_out[pl.ds(at + tile, spare), :] = sums_to(sums, spare, mix_out.shape[1]).astype(mix_out.dtype)
            else:
                to_rows = pl.ds(pl.multiple_of(i * tile, tile), tile)
                mix_out[to_rows, :] = mix
                outs[2 * k + 1][to_rows, :] = sums


def sum_rows(reps):
    return 8 if reps == 2 else 16


def sums_to(sums, spare, width):
    rows = jnp.transpose(jnp.broadcast_to(sums, (sums.shape[0], 128)))[:spare]
    high = rows.astype(jnp.bfloat16).astype(jnp.float32)
    place = lax.broadcasted_iota(jnp.int32, rows.shape, 0)
    rows = jnp.where(place == 0, high, jnp.where(place == 1, rows - high, 0.0))
    if rows.shape[1] == width:
        return rows
    return jnp.concatenate([rows, jnp.zeros((spare, width - rows.shape[1]), jnp.float32)], axis=1)


def sums_from(rows, count):
    rows = rows.astype(jnp.float32)[:, :count]
    return column(rows[:1] + rows[1:2])


def add_labels(table, bias, labels, sets, *, step, pieces, parts, part_rows, reps, where=("all", 0, 1), narrow=False):
    embed_width = labels[0].shape[1] - sets[0][0].shape[1] if pieces else labels[1].shape[1]
    first, received = len(sets[0]) == 2, len(sets[0]) > 4
    spec = (step, pieces, part_rows, len(sets), first, where, reps, received, narrow)
    operands = [bias, *labels]
    aliases, out_shape = {}, []
    kind, _, count = where
    for k, one in enumerate(sets):
        held = one[0].shape[0] // (1 if kind == "all" else reps)
        if kind == "all" and not first:
            aliases[1 + len(operands) + 2] = 2 * k
            aliases[1 + len(operands) + 3] = 2 * k + 1
        operands += one
        if narrow:
            rows = (held // count + sum_rows(reps)) * (reps - 1 if kind == "away" else 1)
            out_shape.append(jax.ShapeDtypeStruct((rows, embed_width), jnp.bfloat16))
        else:
            out_shape.append(jax.ShapeDtypeStruct((held, embed_width), jnp.float32))
            out_shape.append(jax.ShapeDtypeStruct((held, 1), jnp.float32))
    if pieces and kind == "all":
        out_shape.append(jax.ShapeDtypeStruct((8, parts * part_rows), jnp.float32))
    outs = pl.pallas_call(
        functools.partial(accumulate, spec),
        in_specs=[pl.BlockSpec(memory_space=pltpu.SMEM)] + [pl.BlockSpec(memory_space=pltpu.VMEM)] * len(operands),
        out_specs=[pl.BlockSpec(memory_space=pltpu.VMEM)] * len(out_shape),
        out_shape=out_shape,
        input_output_aliases=aliases,
        compiler_params=pltpu.CompilerParams(vmem_limit_bytes=VMEM_LIMIT),
        cost_estimate=pl.CostEstimate(flops=0, bytes_accessed=0, transcendentals=0),
    )(table, *operands)
    if narrow:
        return outs[0]
    totals = [list(outs[2 * k : 2 * k + 2]) for k in range(len(sets))]
    return (totals, outs[-1]) if len(outs) > 2 * len(sets) else totals


def combine(spec, mix_ref, sum_ref, *refs):
    piece, count, shares = spec
    out_ref, held, sem = refs[-3:]
    rows = mix_ref.shape[0] // count
    where = slice(piece * rows, (piece + 1) * rows)
    mix, sums = mix_ref[where, :], sum_ref[where, :]
    for arrays in shares:
        parts, refs = refs[:arrays], refs[arrays:]
        left = rows - sum(ref.shape[0] for ref in parts[:-1])
        mix = mix + joined([ref[...].astype(jnp.float32) for ref in parts[:-1]] + [parts[-1][:left, :].astype(jnp.float32)], 0)
        sums = sums + sums_from(parts[-1][left:, :], rows)
    held[...] = (mix / jnp.sqrt(1.0 + sums)).astype(held.dtype)
    copy = pltpu.make_async_copy(held, out_ref.at[pl.ds(piece * rows, rows), :], sem)
    copy.start()
    copy.wait()


def combined(mix, sums, shares):
    count, out = len(shares), None
    for piece in range(count):
        operands = [mix, sums, *sum(shares[piece], [])]
        in_specs = [pl.BlockSpec(memory_space=pltpu.VMEM)] * len(operands)
        aliases = {}
        if out is not None:
            operands.append(out)
            in_specs.append(pl.BlockSpec(memory_space=pl.ANY))
            aliases = {len(operands) - 1: 0}
        out = pl.pallas_call(
            functools.partial(combine, (piece, count, tuple(len(arrays) for arrays in shares[piece]))),
            in_specs=in_specs,
            out_specs=pl.BlockSpec(memory_space=pl.ANY),
            out_shape=jax.ShapeDtypeStruct(mix.shape, jnp.bfloat16),
            input_output_aliases=aliases,
            scratch_shapes=[pltpu.VMEM((mix.shape[0] // count, mix.shape[1]), jnp.bfloat16), pltpu.SemaphoreType.DMA(())],
            compiler_params=pltpu.CompilerParams(vmem_limit_bytes=VMEM_LIMIT),
            cost_estimate=pl.CostEstimate(flops=COST_PIECE, bytes_accessed=0, transcendentals=0),
        )(*operands)
    return out


def pack(spec, table, weight, embed, bias, out, near, sems):
    offset, rows, part_rows, groups = spec
    width = weight.shape[1]
    group = table[0]
    source = pl.ds(pl.multiple_of(group * part_rows + offset, 16), rows)
    copies = [
        pltpu.make_async_copy(weight.at[source, :], out.at[pl.ds(0, rows), pl.ds(0, width)], sems.at[0]),
        pltpu.make_async_copy(embed.at[source, :], out.at[pl.ds(0, rows), pl.ds(width, embed.shape[1])], sems.at[1]),
    ]
    for copy in copies:
        copy.start()
    if offset == 0:
        copy = pltpu.make_async_copy(bias, near, sems.at[2])
        copy.start()
        copy.wait()
        every = in_one_row(near)
        row = every[:, :part_rows]
        for other in range(1, groups):
            row = jnp.where(group == other, every[:, other * part_rows : (other + 1) * part_rows], row)
        out[rows:, :part_rows] = jnp.broadcast_to(row, (BIAS_ROWS, part_rows)).astype(out.dtype)
        out[rows:, part_rows:] = jnp.zeros((BIAS_ROWS, out.shape[1] - part_rows), out.dtype)
    for copy in copies:
        copy.wait()


def packed_part(table, weight, embed, bias, offset, rows, part_rows, groups, cost):
    width = weight.shape[1] + embed.shape[1]
    return pl.pallas_call(
        functools.partial(pack, (offset, rows, part_rows, groups)),
        in_specs=[pl.BlockSpec(memory_space=pltpu.SMEM)]
        + [pl.BlockSpec(memory_space=pl.ANY)] * 3,
        out_specs=pl.BlockSpec(memory_space=pltpu.VMEM),
        out_shape=jax.ShapeDtypeStruct((rows + (0 if offset else BIAS_ROWS), width), weight.dtype),
        scratch_shapes=[pltpu.VMEM(bias.shape, bias.dtype), pltpu.SemaphoreType.DMA((3,))],
        compiler_params=pltpu.CompilerParams(vmem_limit_bytes=VMEM_LIMIT),
        cost_estimate=pl.CostEstimate(flops=cost, bytes_accessed=0, transcendentals=0),
    )(table, *[pltpu.with_memory_space_constraint(x, pltpu.HBM) for x in (weight, embed, bias)])


def per_device(sizes, documents, block_ids, label_weight, label_bias, label_embed):
    groups, loop, reps = sizes
    cores = 2 if loop % 2 == 0 else 1
    chips = loop // cores
    doc_count = documents.shape[0]
    part_rows = label_weight.shape[0] // groups

    def moved(x, to):
        pairs = []
        for g in range(groups):
            for l in range(loop):
                for r in range(reps):
                    g2, z2, c2, r2 = to(g, l // cores, l % cores, r)
                    there = (g2 % groups, (z2 % chips) * cores + c2 % cores, r2 % reps)
                    number = lambda a: (a[0] * loop + a[1]) * reps + a[2]
                    pairs.append((number((g, l, r)), number(there)))
        return lax.ppermute(x, AXES, pairs)

    along = lambda x: moved(x, lambda g, z, c, r: (g, z + 1, c, r))
    across = lambda x, k: moved(x, lambda g, z, c, r: (g + k, z, c, r))
    other_core = lambda x: moved(x, lambda g, z, c, r: (g, z, c + 1, r))
    other_rep = lambda x, k: moved(x, lambda g, z, c, r: (g, z, c, r + k))

    place = lax.axis_index("loop")
    chip, core = place // cores, place % cores
    entries = [lax.axis_index("groups")]
    entries += [((chip - step) % chips) * cores + core for step in range(chips)]
    entries.append(lax.axis_index("rep"))
    table = jnp.stack(entries).astype(jnp.int32)

    total = sum(SHARES)
    cuts = [part_rows * sum(SHARES[:k]) // total // 16 * 16 for k in range(len(SHARES))] + [part_rows]
    chunks = [(a, b - a) for a, b in zip(cuts, cuts[1:])]
    bias = label_bias.reshape(-1, 128)
    sets = [[documents, block_ids]]
    later = table
    if cores == 2:
        sets.append([other_core(documents), other_core(block_ids)])
        later, sets[1][1] = lax.optimization_barrier((table, sets[1][1]))
    flying = [
        packed_part(
            later if offset else table,
            label_weight,
            label_embed,
            bias,
            offset,
            rows,
            part_rows,
            groups,
            COST_NEXT if offset else 0,
        )
        for offset, rows in chunks
    ]
    call = functools.partial(add_labels, table)
    common = dict(parts=groups, part_rows=part_rows, reps=reps)
    history = [call(bias, [label_weight, label_embed], sets, step=0, pieces=(), **common)]

    def after(x, step, index):
        back = TIES.get(("last" if step + 1 == chips else "first" if step == 1 else "mid", index))
        if back is None or back > step:
            return x
        x, history[step - back] = lax.optimization_barrier((x, history[step - back]))
        return x

    def kernel(pieces, bias, step):
        arrays = [x for _, x in pieces]
        one = [s + t for s, t in zip(sets, history[-1])]
        return call(bias, arrays, one, step=step, pieces=tuple(place for place, _ in pieces), **common)

    final = len(chunks) - 1
    for step in range(1, chips):
        earlier, arrived = (arrived if step > 1 else None), []
        for index, (offset, rows) in enumerate(chunks):
            near = rows * NEAR // 128 // 16 * 16 if step + 1 == chips and index == final and step > 1 else rows
            flying[index] = after(along(flying[index]), step, index)
            pieces = [((0, offset), flying[index])]
            for k in range(1, groups):
                pieces.append(((k, offset), across(flying[index][:near] if near < rows else flying[index], k)))
                if near < rows:
                    pieces.append(((k, offset + near), along(earlier[index][k][1][near:])))
            arrived.append(pieces)
        if step + 1 < chips:
            history.append(kernel(sum(arrived, []), bias, step)[0])
    totals, bias = kernel(sum(arrived[:final], []), bias, chips - 1)
    held = [one + t for one, t in zip(sets, totals)]
    labels = [x for _, x in arrived[final]]
    here = dict(step=chips - 1, pieces=tuple(place for place, _ in arrived[final]), **common)
    call = functools.partial(call, bias)

    tile_docs = doc_count // reps
    halves = HALVES if tile_docs // HALVES >= 128 else 1
    given = [None] * halves
    if cores == 2:
        for h in range(halves):
            given[h] = other_core(call(labels, [held[1]], where=("away", h, halves), narrow=True, **here))
    shares = []
    for h in range(halves):
        one = held[0] + ([given[h]] if cores == 2 else [])
        share = call(labels, [one], where=("away", h, halves), narrow=True, **here)
        stride = share.shape[0] // (reps - 1)
        if h == 0:
            lead = share
        shares.append([[other_rep(share if reps == 2 else share[k * stride - stride : k * stride], k)] for k in range(1, reps)])
    if cores == 2:
        lead, held[1] = lax.optimization_barrier((lead, held[1]))
        for h in range(halves):
            share = call(labels, [held[1]], where=("home", h, halves), narrow=True, **here)
            cut = tile_docs // halves // 2
            shares[h].append([other_core(share[:cut]), other_core(share[cut:])])
    ((home_mix, home_sum),) = call(labels, [held[0]], where=("home", 0, 1), **here)
    return combined(home_mix, home_sum, shares)


def solution(mesh):
    sizes = tuple(mesh.shape[axis] for axis in AXES)
    return jax.shard_map(
        functools.partial(per_device, sizes),
        mesh=mesh,
        in_specs=(
            P(("groups", "loop"), None),
            P(("groups", "loop"), None),
            P(("loop", "rep"), None),
            P(("loop", "rep")),
            P(("loop", "rep"), None),
        ),
        out_specs=P(("groups", "loop", "rep"), None),
        check_vma=False,
    )
```
